256 devices in a mesh: row: 32 (over z, y), col: 8 (over x, core).
Axes of the slice: x: 4, y: 4, z: 8, core: 2. Of those that a mesh axis runs over, the one named last changes fastest.
Arguments:
- window: float32 [131072, 2048], P('row', 'col'), may hold values from -5 to 5
- outer_diag: float32 [131072], P('row'), may hold values from 0.6 to 1.6
- inner_diag: float32 [131072], P('row'), may hold values from 0.6 to 1.6
- column_diag: float32 [2048], P('col'), may hold values from 0.6 to 1.6
Outputs:
- factored: float32 [131072, 2048], P('row', 'col')
The draws below stay inside these ranges and needn't reach their ends.
All inputs are finite; a program needn't handle non-finite values.
Results may differ from the reference program's by a relative error of at most 0.000098.
Values sent between devices are 32-bit elements; how exact they have to be, the bound alone decides.
A program may use at most 128 MiB of HBM per device.

```python
import math
import jax
import jax.numpy as jnp
from jax import lax

SLAB = 1024
PANEL = 256
NROWS = 131072


def draw_window(key, part):
    key = jax.random.fold_in(key, 7)
    noise_scale = 1.0 / math.sqrt(PANEL)
    noise = jnp.clip(jax.random.normal(key, (NROWS, 2 * SLAB), jnp.float32), -6.0, 6.0)
    row_phase = jnp.arange(NROWS)[:, None] % SLAB
    column_phase = jnp.arange(2 * SLAB)[None, :] % SLAB
    return noise * noise_scale + jnp.where(row_phase == column_phase, 2.0, 0.0)


def block_levels(key, extent, split, least, largest):
    factor_of, own = 1.0, jax.random.fold_in(key, 6)
    for dim, blocks in split:
        steps = jnp.exp(jax.random.uniform(jax.random.fold_in(own, dim), (blocks,), jnp.float32, least / len(split), largest / len(split)))
        factor_of = factor_of * jnp.repeat(steps, extent[dim] // blocks).reshape([-1 if axis == dim else 1 for axis in range(len(extent))])
    return factor_of


def setup_inputs(seed: int = 0) -> dict:
    key_list = jax.random.split(jax.random.key(seed), 5)
    window = draw_window(jax.random.fold_in(key_list[4], 71), 0)
    outer_diag = jnp.clip(jnp.exp(math.log(1.6) - 0.98082923 * jax.random.uniform(key_list[1], (NROWS,), jnp.float32) ** block_levels(key_list[1], (NROWS,), ((0, 32),), -0.2, 0.2)), 0.6, 1.6)
    inner_diag = jnp.clip(jnp.exp(math.log(1.6) - 0.98082923 * jax.random.uniform(key_list[2], (NROWS,), jnp.float32) ** block_levels(key_list[2], (NROWS,), ((0, 32),), -0.2, 0.2)), 0.6, 1.6)
    column_diag = jnp.clip(jnp.exp(math.log(1.6) - 0.98082923 * jax.random.uniform(key_list[3], (2 * SLAB,), jnp.float32) ** block_levels(key_list[3], (2 * SLAB,), ((0, 8),), -0.2, 0.2)), 0.6, 1.6)
    return {"window": window, "outer_diag": outer_diag, "inner_diag": inner_diag, "column_diag": column_diag}


root_half = 0.7071067811865476

def direct_factor(block):
    order_size = block.shape[0]
    matrix_now = block
    for pivot_index in range(order_size - 1):
        column_part = matrix_now[pivot_index + 1:, pivot_index] / matrix_now[pivot_index, pivot_index]
        row_part = matrix_now[pivot_index, pivot_index + 1:]
        matrix_now = matrix_now.at[pivot_index + 1:, pivot_index + 1:].add(-column_part[:, None] * row_part[None, :])
        matrix_now = matrix_now.at[pivot_index + 1:, pivot_index].set(column_part)
    return matrix_now

def factor_block(block):
    order_size = block.shape[0]
    if order_size <= 8:
        return direct_factor(block)
    half_size = order_size // 2
    leading = factor_block(block[:half_size, :half_size])
    lower_unit = jnp.tril(leading, -1) + jnp.eye(half_size, dtype=leading.dtype)
    upper_tri = jnp.triu(leading)
    right_strip = jax.scipy.linalg.solve_triangular(lower_unit, block[:half_size, half_size:], lower=True, unit_diagonal=True)
    left_strip = jax.scipy.linalg.solve_triangular(upper_tri.T, block[half_size:, :half_size].T, lower=True).T
    trailing = block[half_size:, half_size:] - jnp.dot(left_strip, right_strip, precision=lax.Precision.HIGHEST)
    trailing = factor_block(trailing)
    top_rows = jnp.concatenate([leading, right_strip], 1)
    bottom_rows = jnp.concatenate([left_strip, trailing], 1)
    return jnp.concatenate([top_rows, bottom_rows], 0)

def reference(window, outer_diag, inner_diag, column_diag):
    total_rows, width_all = window.shape
    scaled = window * outer_diag[:, None]
    half_rows = total_rows // 2
    upper_rows = scaled[:half_rows]
    lower_rows = scaled[half_rows:]
    level_one = jnp.concatenate([upper_rows + lower_rows, upper_rows - lower_rows], 0) * root_half
    scaled = (level_one * inner_diag[:, None]).reshape(2, 2, total_rows // 4, width_all)
    first_quarter = scaled[:, 0]
    second_quarter = scaled[:, 1]
    level_two = jnp.stack([first_quarter + second_quarter, first_quarter - second_quarter], 1).reshape(total_rows, width_all) * root_half
    scaled = level_two * column_diag[None, :]
    left_side = scaled[:, :SLAB]
    right_side = scaled[:, SLAB:]
    mixed = jnp.concatenate([left_side + right_side, left_side - right_side], 1) * root_half
    panel_block = mixed[:, :PANEL]
    packed = factor_block(panel_block[:PANEL])
    lower_unit = jnp.tril(packed, -1) + jnp.eye(PANEL, dtype=packed.dtype)
    upper_tri = jnp.triu(packed)
    lower_part = jax.scipy.linalg.solve_triangular(upper_tri.T, panel_block.T, lower=True).T
    upper_part = jax.scipy.linalg.solve_triangular(lower_unit, mixed[:PANEL], lower=True, unit_diagonal=True)
    rest = mixed - jnp.dot(lower_part, upper_part, precision=lax.Precision.HIGHEST)
    body_rows = jnp.concatenate([lower_part, rest[:, PANEL:]], 1)
    top_rows = jnp.concatenate([packed, upper_part[:, PANEL:]], 1)
    return jnp.concatenate([top_rows, body_rows[PANEL:]], 0)
```

```python
import jax
import jax.numpy as jnp
from jax import lax
from jax.experimental import pallas as pl
from jax.experimental.pallas import tpu as pltpu
from jax.sharding import PartitionSpec as P

MESH = pl.DeviceIdType.MESH
ROOT_HALF = 0.7071067811865476
PANEL = 256
LANES = 128
MEMBERS = 8
CHUNKS = 8
AHEAD = 3
TOP_CHUNKS = CHUNKS // 2
HIGHEST = lax.Precision.HIGHEST


def dot(a, b):
    return jnp.dot(a, b, precision=HIGHEST, preferred_element_type=jnp.float32)


def iota(shape, dim):
    return lax.broadcasted_iota(jnp.int32, shape, dim)


def lu_steps(lu, first, count):
    left = 0 if first < LANES else LANES
    rows, width = PANEL - first, PANEL - left
    lane = iota((1, width), 1) + left
    half_lane = iota((1, LANES), 1) + left
    row_id = iota((rows, 1), 0) + first

    def step(i, carry):
        k = first + i
        pivot_row = lu[pl.ds(k, 1)][:, left:]
        pivot = jnp.sum(jnp.where(half_lane == k, pivot_row[:, :LANES], 0.0), axis=1, keepdims=True)
        column = jnp.sum(
            jnp.where(half_lane == k, lu[first:, left : left + LANES], 0.0), axis=1, keepdims=True
        )
        factor = jnp.where(row_id > k, column / pivot, 0.0)
        lu[first:, left:] = lu[first:, left:] - factor * jnp.where(lane > k, pivot_row, 0.0)
        return carry

    lax.fori_loop(0, count, step, 0)


def invert(lu, unit_upper, low_inv, up_inv):
    i, j = iota((PANEL, PANEL), 0), iota((PANEL, PANEL), 1)
    raw = lu[...]
    diag = jnp.where(i == j, raw, 0.0)
    diag_row = jnp.sum(diag, axis=0, keepdims=True)
    diag_col = jnp.sum(diag, axis=1, keepdims=True)
    lu[...] = jnp.where(i > j, raw / diag_row, raw)
    unit_upper[...] = raw / diag_col
    eye = jnp.where(i == j, 1.0, 0.0)
    low_inv[...] = eye - jnp.where((i == j + 1) & (i % 2 == 1), lu[...], 0.0)
    up_inv[...] = eye - jnp.where((j == i + 1) & (j % 2 == 1), unit_upper[...], 0.0)

    def level(n, carry):
        bi, bj = lax.shift_right_logical(i, n), lax.shift_right_logical(j, n)
        low = jnp.where((bi == bj + 1) & (bi % 2 == 1), lu[...], 0.0)
        up = jnp.where((bj == bi + 1) & (bj % 2 == 1), unit_upper[...], 0.0)
        low_inv[...] -= dot(low_inv[...], dot(low, low_inv[...]))
        up_inv[...] -= dot(up_inv[...], dot(up, up_inv[...]))
        return carry

    lax.fori_loop(1, 8, level, 0)
    up_inv[...] = up_inv[...] / diag_row


def kernel(
    window, outer, inner, cdiag, out,
    d_send, d_recv, d_wide, rx, tx, mixed, panel, result,
    top, a00, lu, unit_upper, low_inv, up_inv, top_out, w,
    s_d, s_rx1, s_tx1, s_rx2, s_tx2, s_prx, s_ptx, s_top, s_aux, s_w, s_wy, s_wtx, s_out,
):
    row, col = lax.axis_index("row"), lax.axis_index("col")
    z, y = row // 4, row % 4
    core = col % 2
    q, xh = row // 8, col // 4
    me = q * 2 + xh
    rows = rx.shape[2]

    def member(mq, mx):
        return (row % 8 + 8 * mq, col % 4 + 4 * mx)

    def remote(src, dst, send, recv, where):
        return pltpu.make_async_remote_copy(src, dst, send, recv, device_id=where, device_id_type=MESH)

    others = [(dq, dx) for dq in range(4) for dx in range(2) if dq or dx]

    def peer(dq, dx):
        return (q + dq) % 4, (xh + dx) % 2

    barrier = pltpu.get_barrier_semaphore()
    partners = [member(*peer(dq, dx)) for dq, dx in others]
    partners += [(row, col // 4 * 4 + (col + n) % 4) for n in range(1, 4)]
    partners += [(row, (col // 4 * 4 + 4) % 8 + (col + n) % 4) for n in range(1, 4)]
    partners += [((z + n) % 8 * 4 + y, col) for n in (1, 3, 5, 7)]
    partners += [(z * 4 + (y + n) % 4, col) for n in range(1, 4)]
    for where in partners:
        pl.semaphore_signal(barrier, inc=1, device_id=where, device_id_type=MESH)
    for p in range(MEMBERS):
        d_send[p, 0:4] = outer[4 * p : 4 * p + 4] * ROOT_HALF
        d_send[p, 4:8] = inner[4 * p : 4 * p + 4] * ROOT_HALF
        d_send[p, 8:10] = cdiag[...] * ROOT_HALF
        d_send[p, 10:16] = jnp.zeros((6, LANES), jnp.float32)
    pl.semaphore_wait(barrier, len(partners))

    pltpu.make_async_copy(d_send.at[me], d_recv.at[me], s_d.at[0]).start()
    for dq, dx in others:
        mq, mx = peer(dq, dx)
        remote(d_send.at[mq * 2 + mx], d_recv.at[me], s_d.at[1], s_d.at[0], member(mq, mx)).start()

    def send_first(k):
        pltpu.make_async_copy(window.at[me, k], rx.at[k, me], s_rx1.at[k]).start()
        for dq, dx in others:
            mq, mx = peer(dq, dx)
            remote(window.at[mq * 2 + mx, k], rx.at[k, me], s_tx1.at[k], s_rx1.at[k], member(mq, mx)).start()

    for k in range(AHEAD):
        send_first(k)

    pltpu.make_async_copy(d_recv, d_recv, s_d.at[0]).wait()
    for n in range(4):
        turned = jnp.transpose(d_recv[2 * n, 0:8])
        for part in range(2):
            for b in range(4):
                lane = 4 * part + b
                d_wide[part * 4 + n, 128 * b : 128 * b + 128] = jnp.broadcast_to(
                    turned[:, lane : lane + 1], (LANES, LANES)
                )

    def mix(k):
        def tile(t, carry):
            r0 = pl.multiple_of(t * 8, 8)
            for h in range(2):
                lanes = slice(h * LANES, h * LANES + LANES)
                od = [d_wide[n, pl.ds(k * rows + r0, 8)] for n in range(4)]
                idg = [d_wide[4 + n, pl.ds(k * rows + r0, 8)] for n in range(4)]
                sides = []
                for side in range(2):
                    x = [rx[k, 2 * n + side, pl.ds(r0, 8), lanes] * od[n] for n in range(4)]
                    a = [x[0] + x[2], x[1] + x[3], x[0] - x[2], x[1] - x[3]]
                    a = [a[n] * idg[n] for n in range(4)]
                    b = [a[0] + a[1], a[0] - a[1], a[2] + a[3], a[2] - a[3]]
                    cd = d_recv[side, 8 + h : 9 + h]
                    sides.append([v * cd for v in b])
                for n in range(4):
                    tx[k, 2 * n, pl.ds(r0, 8), lanes] = sides[0][n] + sides[1][n]
                    tx[k, 2 * n + 1, pl.ds(r0, 8), lanes] = sides[0][n] - sides[1][n]
            return carry

        lax.fori_loop(0, rows // 8, tile, 0)

    def send_second(k, mx):
        for dq in range(4):
            mq = (q + dq) % 4
            src = tx.at[k, mq * 2 + mx]

            def far(src=src, mq=mq):
                remote(src, mixed.at[me, k], s_tx2.at[k], s_rx2.at[k], member(mq, mx)).start()

            if dq:
                far()
            else:
                pl.when(mx != xh)(far)

                @pl.when(mx == xh)
                def _(src=src):
                    pltpu.make_async_copy(src, mixed.at[me, k], s_rx2.at[k]).start()

    half = pl.ds(0, TOP_CHUNKS)

    def tree(src0, src, dst, send, recv, act):
        for column, kids in ((0, ((2, 0), (6, 1), (1, 2))), (2, ((4, 0), (3, 2))), (4, ((5, 2),)), (6, ((7, 2),))):
            @pl.when(col == column)
            def _(column=column, kids=kids):
                for kid, n in kids:
                    act(remote(src0 if column == 0 else src, dst, send.at[n], recv, (row, kid)))

    def start(copy):
        copy.start()

    def wait_send(copy):
        copy.wait_send()

    on_top = row == 0
    for k in range(CHUNKS):
        pltpu.make_async_copy(rx.at[k], rx.at[k], s_rx1.at[k]).wait()
        if k + AHEAD < CHUNKS:
            send_first(k + AHEAD)
        mix(k)
        send_second(k, core)

        if k == TOP_CHUNKS - 1:
            @pl.when(on_top & (col < 4))
            def _():
                remote(tx.at[half, 1], top, s_aux.at[3], s_top.at[0], (row, col + 4)).start()
                pltpu.make_async_copy(tx.at[half, 0], top, s_top.at[0]).start()

            @pl.when(on_top & (col == 0))
            def _():
                pltpu.make_async_copy(tx.at[half, 0], a00, s_top.at[1]).start()
                tree(tx.at[half, 0], a00, a00, s_aux, s_top.at[1], start)

        if k == TOP_CHUNKS:
            @pl.when(on_top)
            def _():
                pltpu.make_async_copy(a00, a00, s_top.at[1]).wait()

                @pl.when(col > 0)
                def _():
                    tree(a00, a00, a00, s_aux, s_top.at[1], start)

                lu[...] = a00[...].reshape(PANEL, PANEL)

        if k >= TOP_CHUNKS:
            @pl.when(on_top)
            def _(k=k):
                lu_steps(lu, 64 * (k - TOP_CHUNKS), 64)

    def send_rest(k, carry):
        send_second(k, 1 - core)
        return carry

    lax.fori_loop(0, CHUNKS, send_rest, 0)

    @pl.when(on_top)
    def _():
        invert(lu, unit_upper, low_inv, up_inv)
        pltpu.make_async_copy(top, top, s_top.at[0]).wait()

        @pl.when(col == 0)
        def _():
            top_out[...] = lu[...]
            w[...] = up_inv[...].reshape(w.shape)

        @pl.when(col > 0)
        def _():
            top_out[...] = dot(low_inv[...], top[...].reshape(PANEL, PANEL))
            w[...] = dot(up_inv[...], top_out[...]).reshape(w.shape)

    def w_scatter(act):
        @pl.when(on_top)
        def _():
            for n in range(1, 4):
                act(remote(w.at[n], w.at[n], s_wtx.at[n - 1], s_w, (n, col)))

    def w_along_z(act):
        @pl.when(z == 0)
        def _():
            for n in range(1, 8):
                act(remote(w.at[y], w.at[y], s_wtx.at[2 + n], s_w, (n * 4 + y, col)))

    def w_along_y(act):
        for n in range(1, 4):
            @pl.when((z > 0) | (y != 4 - n))
            def _(n=n):
                act(remote(w.at[y], w.at[y], s_wtx.at[9 + n], s_wy.at[n - 1], (z * 4 + (y + n) % 4, col)))

    @pl.when(on_top)
    def _():
        w_scatter(start)
        w_along_z(start)
        w_along_y(start)

    def relay(k, carry):
        @pl.when(col == 0)
        def _():
            pltpu.make_async_copy(mixed.at[:, k], mixed.at[:, k], s_rx2.at[k]).wait()

        @pl.when(col > 0)
        def _():
            pltpu.make_async_copy(panel.at[:, k], panel.at[:, k], s_prx.at[k]).wait()

        tree(mixed.at[:, k], panel.at[:, k], panel.at[:, k], s_ptx.at[k], s_prx.at[k], start)
        return carry

    lax.fori_loop(0, CHUNKS, relay, 0)

    @pl.when(row > 0)
    def _():
        pltpu.make_async_copy(w.at[y], w.at[y], s_w).wait()
        w_along_z(start)
        w_along_y(start)
        for n in range(1, 4):
            pltpu.make_async_copy(w.at[0], w.at[0], s_wy.at[n - 1]).wait()

    def finish(k, carry):
        @pl.when(col == 0)
        def _():
            whole = mixed[:, k].reshape(MEMBERS * rows, PANEL)
            result[:, k] = dot(whole, w[...].reshape(PANEL, PANEL)).reshape(MEMBERS, rows, PANEL)

        @pl.when(col > 0)
        def _():
            whole = panel[:, k].reshape(MEMBERS * rows, PANEL)
            product = dot(whole, w[...].reshape(PANEL, PANEL)).reshape(MEMBERS, rows, PANEL)
            pltpu.make_async_copy(mixed.at[:, k], mixed.at[:, k], s_rx2.at[k]).wait()
            result[:, k] = mixed[:, k] - product

        @pl.when(on_top & (k < TOP_CHUNKS))
        def _():
            result[0, k] = top_out[pl.ds(pl.multiple_of(k * rows, rows), rows)]

        pltpu.make_async_copy(result.at[:, k], out.at[:, k], s_out.at[k]).start()
        return carry

    lax.fori_loop(0, CHUNKS, finish, 0)

    seven = pl.ds(0, 7)

    def drain(k, carry):
        pltpu.make_async_copy(rx.at[k, seven], rx.at[k, seven], s_tx1.at[k]).wait()
        pltpu.make_async_copy(tx.at[k, seven], tx.at[k, seven], s_tx2.at[k]).wait()
        tree(mixed.at[:, k], panel.at[:, k], panel.at[:, k], s_ptx.at[k], s_prx.at[k], wait_send)
        pltpu.make_async_copy(result.at[:, k], out.at[:, k], s_out.at[k]).wait()
        return carry

    lax.fori_loop(0, CHUNKS, drain, 0)
    pltpu.make_async_copy(d_recv.at[seven], d_recv.at[seven], s_d.at[1]).wait()

    @pl.when(on_top & (col < 4))
    def _():
        remote(tx.at[half, 1], top, s_aux.at[3], s_top.at[0], (row, col + 4)).wait_send()

    @pl.when(on_top)
    def _():
        tree(tx.at[half, 0], a00, a00, s_aux, s_top.at[1], wait_send)

    w_scatter(wait_send)
    w_along_z(wait_send)
    w_along_y(wait_send)


def local(window, outer_diag, inner_diag, column_diag):
    local_rows, local_cols = window.shape
    rows = local_rows // (MEMBERS * CHUNKS)
    pieces = (MEMBERS, CHUNKS, rows, local_cols)
    f32 = jnp.float32
    dma = pltpu.SemaphoreType.DMA
    square = pltpu.VMEM((PANEL, PANEL), f32)
    quarters = pltpu.VMEM((4, PANEL // 4, PANEL), f32)
    vmem = pl.BlockSpec(memory_space=pltpu.VMEM)
    anywhere = pl.BlockSpec(memory_space=pl.ANY)
    factored = pl.pallas_call(
        kernel,
        out_shape=jax.ShapeDtypeStruct(pieces, f32),
        in_specs=[anywhere, vmem, vmem, vmem],
        out_specs=anywhere,
        scratch_shapes=[
            pltpu.VMEM((MEMBERS, 16, LANES), f32),
            pltpu.VMEM((MEMBERS, 16, LANES), f32),
            pltpu.VMEM((8, local_rows // MEMBERS, LANES), f32),
            pltpu.VMEM((CHUNKS, MEMBERS, rows, local_cols), f32),
            pltpu.VMEM((CHUNKS, MEMBERS, rows, local_cols), f32),
            pltpu.VMEM(pieces, f32),
            pltpu.VMEM(pieces, f32),
            pltpu.VMEM(pieces, f32),
            quarters,
            quarters,
            square,
            square,
            square,
            square,
            square,
            quarters,
            dma((2,)),
            dma((CHUNKS,)),
            dma((CHUNKS,)),
            dma((CHUNKS,)),
            dma((CHUNKS,)),
            dma((CHUNKS,)),
            dma((CHUNKS, 3)),
            dma((2,)),
            dma((4,)),
            dma,
            dma((3,)),
            dma((13,)),
            dma((CHUNKS,)),
        ],
        compiler_params=pltpu.CompilerParams(
            collective_id=0, has_side_effects=True, vmem_limit_bytes=48 * 2**20
        ),
        name="butterfly_lu",
    )(
        window.reshape(pieces),
        outer_diag.reshape(local_rows // LANES, LANES),
        inner_diag.reshape(local_rows // LANES, LANES),
        column_diag.reshape(local_cols // LANES, LANES),
    )
    return factored.reshape(local_rows, local_cols)


def solution(mesh):
    in_specs = (P("row", "col"), P("row"), P("row"), P("col"))
    return jax.shard_map(
        local, mesh=mesh, in_specs=in_specs, out_specs=P("row", "col"), check_vma=False
    )
```

```python
import jax
import jax.numpy as jnp
from jax import lax
from jax.experimental import pallas as pl
from jax.experimental.pallas import tpu as pltpu
from jax.sharding import PartitionSpec as P

MESH = pl.DeviceIdType.MESH
ROOT_HALF = 0.7071067811865476
PANEL = 256
LANES = 128
MEMBERS = 8
CHUNKS = 8
AHEAD = 8
TOP_CHUNKS = CHUNKS // 2
HIGHEST = lax.Precision.HIGHEST


def dot(a, b):
    return jnp.dot(a, b, precision=HIGHEST, preferred_element_type=jnp.float32)


def iota(shape, dim):
    return lax.broadcasted_iota(jnp.int32, shape, dim)


def lu_steps(lu, first, count):
    left = 0 if first < LANES else LANES
    rows, width = PANEL - first, PANEL - left
    lane = iota((1, width), 1) + left
    half_lane = iota((1, LANES), 1) + left
    row_id = iota((rows, 1), 0) + first

    def step(i, carry):
        k = first + i
        pivot_row = lu[pl.ds(k, 1)][:, left:]
        pivot = jnp.sum(jnp.where(half_lane == k, pivot_row[:, :LANES], 0.0), axis=1, keepdims=True)
        column = jnp.sum(
            jnp.where(half_lane == k, lu[first:, left : left + LANES], 0.0), axis=1, keepdims=True
        )
        factor = jnp.where(row_id > k, column / pivot, 0.0)
        lu[first:, left:] = lu[first:, left:] - factor * jnp.where(lane > k, pivot_row, 0.0)
        return carry

    lax.fori_loop(0, count, step, 0)


def invert(lu, unit_upper, low_inv, up_inv):
    i, j = iota((PANEL, PANEL), 0), iota((PANEL, PANEL), 1)
    raw = lu[...]
    diag = jnp.where(i == j, raw, 0.0)
    diag_row = jnp.sum(diag, axis=0, keepdims=True)
    diag_col = jnp.sum(diag, axis=1, keepdims=True)
    lu[...] = jnp.where(i > j, raw / diag_row, raw)
    unit_upper[...] = raw / diag_col
    eye = jnp.where(i == j, 1.0, 0.0)
    low_inv[...] = eye - jnp.where((i == j + 1) & (i % 2 == 1), lu[...], 0.0)
    up_inv[...] = eye - jnp.where((j == i + 1) & (j % 2 == 1), unit_upper[...], 0.0)

    def level(n, carry):
        bi, bj = lax.shift_right_logical(i, n), lax.shift_right_logical(j, n)
        low = jnp.where((bi == bj + 1) & (bi % 2 == 1), lu[...], 0.0)
        up = jnp.where((bj == bi + 1) & (bj % 2 == 1), unit_upper[...], 0.0)
        low_inv[...] -= dot(low_inv[...], dot(low, low_inv[...]))
        up_inv[...] -= dot(up_inv[...], dot(up, up_inv[...]))
        return carry

    lax.fori_loop(1, 8, level, 0)
    up_inv[...] = up_inv[...] / diag_row


def kernel(
    window, outer, inner, cdiag, out,
    d_send, d_recv, d_wide, rx, tx, mixed, panel, result,
    top, a00, lu, unit_upper, low_inv, up_inv, top_out, w,
    s_d, s_rx1, s_tx1, s_rx2, s_tx2, s_prx, s_ptx, s_top, s_aux, s_w, s_wy, s_wtx, s_out,
):
    row, col = lax.axis_index("row"), lax.axis_index("col")
    z, y = row // 4, row % 4
    core = col % 2
    q, xh = row // 8, col // 4
    me = q * 2 + xh
    rows = rx.shape[2]

    def member(mq, mx):
        return (row % 8 + 8 * mq, col % 4 + 4 * mx)

    def remote(src, dst, send, recv, where):
        return pltpu.make_async_remote_copy(src, dst, send, recv, device_id=where, device_id_type=MESH)

    others = [(dq, dx) for dq in range(4) for dx in range(2) if dq or dx]

    def peer(dq, dx):
        return (q + dq) % 4, (xh + dx) % 2

    barrier = pltpu.get_barrier_semaphore()
    partners = [member(*peer(dq, dx)) for dq, dx in others]
    partners += [(row, col // 4 * 4 + (col + n) % 4) for n in range(1, 4)]
    partners += [(row, (col // 4 * 4 + 4) % 8 + (col + n) % 4) for n in range(1, 4)]
    partners += [((z + n) % 8 * 4 + y, col) for n in (1, 3, 5, 7)]
    partners += [(z * 4 + (y + n) % 4, col) for n in range(1, 4)]
    for where in partners:
        pl.semaphore_signal(barrier, inc=1, device_id=where, device_id_type=MESH)
    for p in range(MEMBERS):
        d_send[p, 0:4] = outer[4 * p : 4 * p + 4] * ROOT_HALF
        d_send[p, 4:8] = inner[4 * p : 4 * p + 4] * ROOT_HALF
        d_send[p, 8:10] = cdiag[...] * ROOT_HALF
        d_send[p, 10:16] = jnp.zeros((6, LANES), jnp.float32)
    pl.semaphore_wait(barrier, len(partners))

    pltpu.make_async_copy(d_send.at[me], d_recv.at[me], s_d.at[0]).start()
    for dq, dx in others:
        mq, mx = peer(dq, dx)
        remote(d_send.at[mq * 2 + mx], d_recv.at[me], s_d.at[1], s_d.at[0], member(mq, mx)).start()

    def send_first(k):
        pltpu.make_async_copy(window.at[me, k], rx.at[k, me], s_rx1.at[k]).start()
        for dq, dx in others:
            mq, mx = peer(dq, dx)
            remote(window.at[mq * 2 + mx, k], rx.at[k, me], s_tx1.at[k], s_rx1.at[k], member(mq, mx)).start()

    for k in range(AHEAD):
        send_first(k)

    pltpu.make_async_copy(d_recv, d_recv, s_d.at[0]).wait()
    for n in range(4):
        turned = jnp.transpose(d_recv[2 * n, 0:8])
        for part in range(2):
            for b in range(4):
                lane = 4 * part + b
                d_wide[part * 4 + n, 128 * b : 128 * b + 128] = jnp.broadcast_to(
                    turned[:, lane : lane + 1], (LANES, LANES)
                )

    def mix(k):
        def tile(t, carry):
            r0 = pl.multiple_of(t * 8, 8)
            for h in range(2):
                lanes = slice(h * LANES, h * LANES + LANES)
                od = [d_wide[n, pl.ds(k * rows + r0, 8)] for n in range(4)]
                idg = [d_wide[4 + n, pl.ds(k * rows + r0, 8)] for n in range(4)]
                sides = []
                for side in range(2):
                    x = [rx[k, 2 * n + side, pl.ds(r0, 8), lanes] * od[n] for n in range(4)]
                    a = [x[0] + x[2], x[1] + x[3], x[0] - x[2], x[1] - x[3]]
                    a = [a[n] * idg[n] for n in range(4)]
                    b = [a[0] + a[1], a[0] - a[1], a[2] + a[3], a[2] - a[3]]
                    cd = d_recv[side, 8 + h : 9 + h]
                    sides.append([v * cd for v in b])
                for n in range(4):
                    tx[k, 2 * n, pl.ds(r0, 8), lanes] = sides[0][n] + sides[1][n]
                    tx[k, 2 * n + 1, pl.ds(r0, 8), lanes] = sides[0][n] - sides[1][n]
            return carry

        lax.fori_loop(0, rows // 8, tile, 0)

    def send_second(k, mx):
        for dq in range(4):
            mq = (q + dq) % 4
            src = tx.at[k, mq * 2 + mx]

            def far(src=src, mq=mq):
                remote(src, mixed.at[me, k], s_tx2.at[k], s_rx2.at[k], member(mq, mx)).start()

            if dq:
                far()
            else:
                pl.when(mx != xh)(far)

                @pl.when(mx == xh)
                def _(src=src):
                    pltpu.make_async_copy(src, mixed.at[me, k], s_rx2.at[k]).start()

    half = pl.ds(0, TOP_CHUNKS)

    def tree(src0, src, dst, send, recv, act):
        for column, kids in ((0, ((2, 0), (6, 1), (1, 2))), (2, ((4, 0), (3, 2))), (4, ((5, 2),)), (6, ((7, 2),))):
            @pl.when(col == column)
            def _(column=column, kids=kids):
                for kid, n in kids:
                    act(remote(src0 if column == 0 else src, dst, send.at[n], recv, (row, kid)))

    def start(copy):
        copy.start()

    def wait_send(copy):
        copy.wait_send()

    on_top = row == 0
    for k in range(CHUNKS):
        pltpu.make_async_copy(rx.at[k], rx.at[k], s_rx1.at[k]).wait()
        if k + AHEAD < CHUNKS:
            send_first(k + AHEAD)
        mix(k)
        send_second(k, core)

        if k == TOP_CHUNKS - 1:
            @pl.when(on_top & (col < 4))
            def _():
                remote(tx.at[half, 1], top, s_aux.at[3], s_top.at[0], (row, col + 4)).start()
                pltpu.make_async_copy(tx.at[half, 0], top, s_top.at[0]).start()

            @pl.when(on_top & (col == 0))
            def _():
                pltpu.make_async_copy(tx.at[half, 0], a00, s_top.at[1]).start()
                tree(tx.at[half, 0], a00, a00, s_aux, s_top.at[1], start)

        if k == TOP_CHUNKS:
            @pl.when(on_top)
            def _():
                pltpu.make_async_copy(a00, a00, s_top.at[1]).wait()

                @pl.when(col > 0)
                def _():
                    tree(a00, a00, a00, s_aux, s_top.at[1], start)

                lu[...] = a00[...].reshape(PANEL, PANEL)

        if k >= TOP_CHUNKS:
            @pl.when(on_top)
            def _(k=k):
                lu_steps(lu, 64 * (k - TOP_CHUNKS), 64)

    def send_rest(k, carry):
        send_second(k, 1 - core)
        return carry

    lax.fori_loop(0, CHUNKS, send_rest, 0)

    @pl.when(on_top)
    def _():
        invert(lu, unit_upper, low_inv, up_inv)
        pltpu.make_async_copy(top, top, s_top.at[0]).wait()

        @pl.when(col == 0)
        def _():
            top_out[...] = lu[...]
            w[...] = up_inv[...].reshape(w.shape)

        @pl.when(col > 0)
        def _():
            top_out[...] = dot(low_inv[...], top[...].reshape(PANEL, PANEL))
            w[...] = dot(up_inv[...], top_out[...]).reshape(w.shape)

    def w_scatter(act):
        @pl.when(on_top)
        def _():
            for n in range(1, 4):
                act(remote(w.at[n], w.at[n], s_wtx.at[n - 1], s_w, (n, col)))

    def w_along_z(act):
        @pl.when(z == 0)
        def _():
            for n in range(1, 8):
                act(remote(w.at[y], w.at[y], s_wtx.at[2 + n], s_w, (n * 4 + y, col)))

    def w_along_y(act):
        for n in range(1, 4):
            @pl.when((z > 0) | (y != 4 - n))
            def _(n=n):
                act(remote(w.at[y], w.at[y], s_wtx.at[9 + n], s_wy.at[n - 1], (z * 4 + (y + n) % 4, col)))

    @pl.when(on_top)
    def _():
        w_scatter(start)
        w_along_z(start)
        w_along_y(start)

    def relay(k, carry):
        @pl.when(col == 0)
        def _():
            pltpu.make_async_copy(mixed.at[:, k], mixed.at[:, k], s_rx2.at[k]).wait()

        @pl.when(col > 0)
        def _():
            pltpu.make_async_copy(panel.at[:, k], panel.at[:, k], s_prx.at[k]).wait()

        tree(mixed.at[:, k], panel.at[:, k], panel.at[:, k], s_ptx.at[k], s_prx.at[k], start)
        return carry

    lax.fori_loop(0, CHUNKS, relay, 0)

    @pl.when(row > 0)
    def _():
        pltpu.make_async_copy(w.at[y], w.at[y], s_w).wait()
        w_along_z(start)
        w_along_y(start)
        for n in range(1, 4):
            pltpu.make_async_copy(w.at[0], w.at[0], s_wy.at[n - 1]).wait()

    def finish(k, carry):
        @pl.when(col == 0)
        def _():
            whole = mixed[:, k].reshape(MEMBERS * rows, PANEL)
            result[:, k] = dot(whole, w[...].reshape(PANEL, PANEL)).reshape(MEMBERS, rows, PANEL)

        @pl.when(col > 0)
        def _():
            whole = panel[:, k].reshape(MEMBERS * rows, PANEL)
            product = dot(whole, w[...].reshape(PANEL, PANEL)).reshape(MEMBERS, rows, PANEL)
            pltpu.make_async_copy(mixed.at[:, k], mixed.at[:, k], s_rx2.at[k]).wait()
            result[:, k] = mixed[:, k] - product

        @pl.when(on_top & (k < TOP_CHUNKS))
        def _():
            result[0, k] = top_out[pl.ds(pl.multiple_of(k * rows, rows), rows)]

        pltpu.make_async_copy(result.at[:, k], out.at[:, k], s_out.at[k]).start()
        return carry

    lax.fori_loop(0, CHUNKS, finish, 0)

    seven = pl.ds(0, 7)

    def drain(k, carry):
        pltpu.make_async_copy(rx.at[k, seven], rx.at[k, seven], s_tx1.at[k]).wait()
        pltpu.make_async_copy(tx.at[k, seven], tx.at[k, seven], s_tx2.at[k]).wait()
        tree(mixed.at[:, k], panel.at[:, k], panel.at[:, k], s_ptx.at[k], s_prx.at[k], wait_send)
        pltpu.make_async_copy(result.at[:, k], out.at[:, k], s_out.at[k]).wait()
        return carry

    lax.fori_loop(0, CHUNKS, drain, 0)
    pltpu.make_async_copy(d_recv.at[seven], d_recv.at[seven], s_d.at[1]).wait()

    @pl.when(on_top & (col < 4))
    def _():
        remote(tx.at[half, 1], top, s_aux.at[3], s_top.at[0], (row, col + 4)).wait_send()

    @pl.when(on_top)
    def _():
        tree(tx.at[half, 0], a00, a00, s_aux, s_top.at[1], wait_send)

    w_scatter(wait_send)
    w_along_z(wait_send)
    w_along_y(wait_send)


def local(window, outer_diag, inner_diag, column_diag):
    local_rows, local_cols = window.shape
    rows = local_rows // (MEMBERS * CHUNKS)
    pieces = (MEMBERS, CHUNKS, rows, local_cols)
    f32 = jnp.float32
    dma = pltpu.SemaphoreType.DMA
    square = pltpu.VMEM((PANEL, PANEL), f32)
    quarters = pltpu.VMEM((4, PANEL // 4, PANEL), f32)
    vmem = pl.BlockSpec(memory_space=pltpu.VMEM)
    anywhere = pl.BlockSpec(memory_space=pl.ANY)
    factored = pl.pallas_call(
        kernel,
        out_shape=jax.ShapeDtypeStruct(pieces, f32),
        in_specs=[anywhere, vmem, vmem, vmem],
        out_specs=anywhere,
        scratch_shapes=[
            pltpu.VMEM((MEMBERS, 16, LANES), f32),
            pltpu.VMEM((MEMBERS, 16, LANES), f32),
            pltpu.VMEM((8, local_rows // MEMBERS, LANES), f32),
            pltpu.VMEM((CHUNKS, MEMBERS, rows, local_cols), f32),
            pltpu.VMEM((CHUNKS, MEMBERS, rows, local_cols), f32),
            pltpu.VMEM(pieces, f32),
            pltpu.VMEM(pieces, f32),
            pltpu.VMEM(pieces, f32),
            quarters,
            quarters,
            square,
            square,
            square,
            square,
            square,
            quarters,
            dma((2,)),
            dma((CHUNKS,)),
            dma((CHUNKS,)),
            dma((CHUNKS,)),
            dma((CHUNKS,)),
            dma((CHUNKS,)),
            dma((CHUNKS, 3)),
            dma((2,)),
            dma((4,)),
            dma,
            dma((3,)),
            dma((13,)),
            dma((CHUNKS,)),
        ],
        compiler_params=pltpu.CompilerParams(
            collective_id=0, has_side_effects=True, vmem_limit_bytes=48 * 2**20
        ),
        name="butterfly_lu",
    )(
        window.reshape(pieces),
        outer_diag.reshape(local_rows // LANES, LANES),
        inner_diag.reshape(local_rows // LANES, LANES),
        column_diag.reshape(local_cols // LANES, LANES),
    )
    return factored.reshape(local_rows, local_cols)


def solution(mesh):
    in_specs = (P("row", "col"), P("row"), P("row"), P("col"))
    return jax.shard_map(
        local, mesh=mesh, in_specs=in_specs, out_specs=P("row", "col"), check_vma=False
    )
```

```python
import jax
import jax.numpy as jnp
from jax import lax
from jax.experimental import pallas as pl
from jax.experimental.pallas import tpu as pltpu
from jax.sharding import PartitionSpec as P

MESH = pl.DeviceIdType.MESH
ROOT_HALF = 0.7071067811865476
PANEL = 256
LANES = 128
MEMBERS = 8
CHUNKS = 8
W_AT = 4
TOP_CHUNKS = CHUNKS // 2
HIGHEST = lax.Precision.HIGHEST


def dot(a, b):
    return jnp.dot(a, b, precision=HIGHEST, preferred_element_type=jnp.float32)


def iota(shape, dim):
    return lax.broadcasted_iota(jnp.int32, shape, dim)


def lu_steps(lu, first, count):
    left = 0 if first < LANES else LANES
    rows, width = PANEL - first, PANEL - left
    lane = iota((1, width), 1) + left
    half_lane = iota((1, LANES), 1) + left
    row_id = iota((rows, 1), 0) + first

    def step(i, carry):
        k = first + i
        pivot_row = lu[pl.ds(k, 1)][:, left:]
        pivot = jnp.sum(jnp.where(half_lane == k, pivot_row[:, :LANES], 0.0), axis=1, keepdims=True)
        column = jnp.sum(
            jnp.where(half_lane == k, lu[first:, left : left + LANES], 0.0), axis=1, keepdims=True
        )
        factor = jnp.where(row_id > k, column / pivot, 0.0)
        lu[first:, left:] = lu[first:, left:] - factor * jnp.where(lane > k, pivot_row, 0.0)
        return carry

    lax.fori_loop(0, count, step, 0)


def invert(lu, unit_upper, low_inv, up_inv):
    i, j = iota((PANEL, PANEL), 0), iota((PANEL, PANEL), 1)
    raw = lu[...]
    diag = jnp.where(i == j, raw, 0.0)
    diag_row = jnp.sum(diag, axis=0, keepdims=True)
    diag_col = jnp.sum(diag, axis=1, keepdims=True)
    lu[...] = jnp.where(i > j, raw / diag_row, raw)
    unit_upper[...] = raw / diag_col
    eye = jnp.where(i == j, 1.0, 0.0)
    low_inv[...] = eye - jnp.where((i == j + 1) & (i % 2 == 1), lu[...], 0.0)
    up_inv[...] = eye - jnp.where((j == i + 1) & (j % 2 == 1), unit_upper[...], 0.0)

    def level(n, carry):
        bi, bj = lax.shift_right_logical(i, n), lax.shift_right_logical(j, n)
        low = jnp.where((bi == bj + 1) & (bi % 2 == 1), lu[...], 0.0)
        up = jnp.where((bj == bi + 1) & (bj % 2 == 1), unit_upper[...], 0.0)
        low_inv[...] -= dot(low_inv[...], dot(low, low_inv[...]))
        up_inv[...] -= dot(up_inv[...], dot(up, up_inv[...]))
        return carry

    lax.fori_loop(1, 8, level, 0)
    up_inv[...] = up_inv[...] / diag_row


def kernel(
    window, outer_hbm, inner_hbm, cdiag_hbm, out,
    outer, inner, cdiag, d_send, d_recv, d_wide, rx, tx, mixed, panel, result,
    top, a00, lu, unit_upper, low_inv, up_inv, top_out, w,
    s_d, s_rx1, s_tx1, s_rx2, s_tx2, s_pa, s_pb, s_ptx, s_top, s_aux, s_w, s_wy, s_wtx, s_out, s_in,
):
    row, col = lax.axis_index("row"), lax.axis_index("col")
    z, y = row // 4, row % 4
    core = col % 2
    q, xh = row // 8, col // 4
    me = q * 2 + xh
    rows = rx.shape[2]

    def member(mq, mx):
        return (row % 8 + 8 * mq, col % 4 + 4 * mx)

    def remote(src, dst, send, recv, where):
        return pltpu.make_async_remote_copy(src, dst, send, recv, device_id=where, device_id_type=MESH)

    others = [(dq, dx) for dq in range(4) for dx in range(2) if dq or dx]

    def turned_q(dq):
        return (q, q + 1 - 2 * (q % 2), (q + 2) % 4, 3 - q)[dq]

    def peer(dq, dx):
        return turned_q(dq), (xh + dx) % 2

    loads = [
        pltpu.make_async_copy(src, dst, s_in.at[n])
        for n, (src, dst) in enumerate(((outer_hbm, outer), (inner_hbm, inner), (cdiag_hbm, cdiag)))
    ]
    for load in loads:
        load.start()

    barrier = pltpu.get_barrier_semaphore()
    partners = [member(*peer(dq, dx)) for dq, dx in others]
    partners += [(row, col // 4 * 4 + (col + n) % 4) for n in range(1, 4)]
    partners += [(row, (col // 4 * 4 + 4) % 8 + (col + n) % 4) for n in range(1, 4)]
    partners += [((z + n) % 8 * 4 + y, col) for n in (1, 3, 5, 7)]
    partners += [(z * 4 + (y + n) % 4, col) for n in range(1, 4)]
    for where in partners:
        pl.semaphore_signal(barrier, inc=1, device_id=where, device_id_type=MESH)
    for load in loads:
        load.wait()
    for p in range(MEMBERS):
        d_send[p, 0:4] = outer[4 * p : 4 * p + 4] * ROOT_HALF
        d_send[p, 4:8] = inner[4 * p : 4 * p + 4] * ROOT_HALF
        d_send[p, 8:10] = cdiag[...] * ROOT_HALF
        d_send[p, 10:16] = jnp.zeros((6, LANES), jnp.float32)
    pl.semaphore_wait(barrier, len(partners))

    pltpu.make_async_copy(d_send.at[me], d_recv.at[me], s_d.at[0]).start()
    for dq, dx in others:
        mq, mx = peer(dq, dx)
        remote(d_send.at[mq * 2 + mx], d_recv.at[me], s_d.at[1], s_d.at[0], member(mq, mx)).start()

    def send_first(k):
        pltpu.make_async_copy(window.at[q, xh, k], rx.at[k, me], s_rx1.at[k]).start()
        for dq, dx in others:
            mq, mx = peer(dq, dx)
            remote(window.at[mq, mx, k], rx.at[k, me], s_tx1.at[k], s_rx1.at[k], member(mq, mx)).start()

    for k in range(CHUNKS):
        send_first(k)

    pltpu.make_async_copy(d_recv, d_recv, s_d.at[0]).wait()
    for n in range(4):
        turned = jnp.transpose(d_recv[2 * n, 0:8])
        for part in range(2):
            for b in range(4):
                lane = 4 * part + b
                d_wide[part * 4 + n, 128 * b : 128 * b + 128] = jnp.broadcast_to(
                    turned[:, lane : lane + 1], (LANES, LANES)
                )

    def mix(k):
        def tile(t, carry):
            r0 = pl.multiple_of(t * 8, 8)
            for h in range(2):
                lanes = slice(h * LANES, h * LANES + LANES)
                od = [d_wide[n, pl.ds(k * rows + r0, 8)] for n in range(4)]
                idg = [d_wide[4 + n, pl.ds(k * rows + r0, 8)] for n in range(4)]
                sides = []
                for side in range(2):
                    x = [rx[k, 2 * n + side, pl.ds(r0, 8), lanes] * od[n] for n in range(4)]
                    a = [x[0] + x[2], x[1] + x[3], x[0] - x[2], x[1] - x[3]]
                    a = [a[n] * idg[n] for n in range(4)]
                    b = [a[0] + a[1], a[0] - a[1], a[2] + a[3], a[2] - a[3]]
                    cd = d_recv[side, 8 + h : 9 + h]
                    sides.append([v * cd for v in b])
                for n in range(4):
                    tx[k, 2 * n, pl.ds(r0, 8), lanes] = sides[0][n] + sides[1][n]
                    tx[k, 2 * n + 1, pl.ds(r0, 8), lanes] = sides[0][n] - sides[1][n]
            return carry

        lax.fori_loop(0, rows // 8, tile, 0)

    panel_group = col % 4 == 0

    def send_second(k, mx):
        here = panel_group & (xh == 1) & (mx == 0)
        for dq in range(4):
            mq = turned_q(dq)
            src = tx.at[k, mq * 2 + mx]

            def far(src=src, mq=mq):
                remote(src, mixed.at[q, xh, k], s_tx2.at[k], s_rx2.at[k], member(mq, mx)).start()

            def near(src=src, mq=mq):
                remote(src, panel.at[q, xh, k], s_tx2.at[k], s_pb.at[k], member(mq, 1)).start()

            if dq:
                pl.when(here)(near)
                pl.when(jnp.logical_not(here))(far)
            else:
                pl.when((mx != xh) & jnp.logical_not(here))(far)

                @pl.when(here)
                def _(src=src):
                    pltpu.make_async_copy(src, panel.at[q, xh, k], s_pb.at[k]).start()

                @pl.when(mx == xh)
                def _(src=src):
                    pltpu.make_async_copy(src, mixed.at[q, xh, k], s_rx2.at[k]).start()

    half = pl.ds(0, TOP_CHUNKS)

    def spread_a00(src0, act):
        for column, kids in ((0, (4, 2, 6, 1)), (2, (3,)), (4, (5,)), (6, (7,))):
            @pl.when(col == column)
            def _(column=column, kids=kids):
                for n, kid in enumerate(kids):
                    act(remote(src0 if column == 0 else a00, a00, s_aux.at[n], s_top.at[1], (row, kid)))

    def start(copy):
        copy.start()

    def wait_send(copy):
        copy.wait_send()

    on_top = row == 0

    def take_a00():
        pltpu.make_async_copy(a00, a00, s_top.at[1]).wait()

        @pl.when(col > 0)
        def _():
            spread_a00(a00, start)

        lu[...] = a00[...].reshape(PANEL, PANEL)

    def solve_top():
        pltpu.make_async_copy(top, top, s_top.at[0]).wait()

        @pl.when(col == 0)
        def _():
            top_out[...] = lu[...]
            w[...] = up_inv[...].reshape(w.shape)

        @pl.when(col > 0)
        def _():
            top_out[...] = dot(low_inv[...], top[...].reshape(PANEL, PANEL))
            w[...] = dot(up_inv[...], top_out[...]).reshape(w.shape)

    def w_scatter(act):
        @pl.when(on_top)
        def _():
            for n in range(1, 4):
                act(remote(w.at[n], w.at[n], s_wtx.at[n - 1], s_w, (n, col)))

    def w_along_z(act):
        @pl.when(z == 0)
        def _():
            for n in range(1, 8):
                act(remote(w.at[y], w.at[y], s_wtx.at[2 + n], s_w, (n * 4 + y, col)))

    def w_along_y(act):
        for n in range(1, 4):
            @pl.when((z > 0) | (y != 4 - n))
            def _(n=n):
                act(remote(w.at[y], w.at[y], s_wtx.at[9 + n], s_wy.at[n - 1], (z * 4 + (y + n) % 4, col)))

    def top_rows():
        @pl.when(on_top & (col < 4))
        def _():
            remote(tx.at[half, 1], top, s_aux.at[4], s_top.at[0], (row, col + 4)).start()
            pltpu.make_async_copy(tx.at[half, 0], top, s_top.at[0]).start()

        @pl.when(on_top & (col == 0))
        def _():
            pltpu.make_async_copy(tx.at[half, 0], a00, s_top.at[1]).start()
            spread_a00(tx.at[half, 0], start)

    def w_from_top():
        invert(lu, unit_upper, low_inv, up_inv)
        solve_top()
        w_scatter(start)
        w_along_z(start)
        w_along_y(start)

    def w_onward():
        @pl.when(row > 0)
        def _():
            pltpu.make_async_copy(w.at[y], w.at[y], s_w).wait()
            w_along_z(start)
            w_along_y(start)

    def even_of(ref, k):
        return ref.at[:, 0, k]

    def odd_of(ref, k):
        return ref.at[:, 1, k]

    def panel_even(column, k):
        src = even_of(mixed if column == 0 else panel, k)
        kids = {0: (2, 6, 1), 2: (3, 4)[: 2 - k % 2], 4: (5,), 6: (7, 4)[: 1 + k % 2]}[column]
        return [remote(src, even_of(panel, k), s_ptx.at[k, n], s_pa.at[k], (row, kid)) for n, kid in enumerate(kids)]

    def panel_odd(column, k):
        src = odd_of(mixed if column == 0 else panel, k)
        kids = {0: (1,), 2: (3, 0)[: 2 - k % 2], 4: (2, 6, 5), 6: (7, 0)[: 1 + k % 2]}[column]
        return [
            remote(src, odd_of(mixed if kid == 0 else panel, k), s_ptx.at[k, 4 + n], s_pb.at[k], (row, kid))
            for n, kid in enumerate(kids)
        ]

    def await_even(k):
        pltpu.make_async_copy(even_of(panel, k), even_of(panel, k), s_pa.at[k]).wait()

    def await_odd(k):
        pltpu.make_async_copy(odd_of(panel, k), odd_of(panel, k), s_pb.at[k]).wait()

    def send_even(column, k):
        for copy in panel_even(column, k):
            copy.start()

    def send_odd(column, k):
        for copy in panel_odd(column, k):
            copy.start()

    def send_slab(mx):
        def body(k, carry):
            send_second(k, mx)
            return carry

        lax.fori_loop(0, CHUNKS, body, 0)

    for k in range(CHUNKS):
        pltpu.make_async_copy(rx.at[k], rx.at[k], s_rx1.at[k]).wait()
        mix(k)
        send_second(k, core)
        if k == TOP_CHUNKS - 1:
            top_rows()
        if k == TOP_CHUNKS:
            pl.when(on_top)(take_a00)
        if k >= TOP_CHUNKS:
            @pl.when(on_top)
            def _(k=k):
                lu_steps(lu, 64 * (k - TOP_CHUNKS), 64)

    pl.when(on_top)(w_from_top)
    @pl.when(col == 0)
    def _():
        for k in range(CHUNKS):
            if k == W_AT:
                pl.when(z == 0)(w_onward)
            pltpu.make_async_copy(even_of(mixed, k), even_of(mixed, k), s_rx2.at[k]).wait()
            send_even(0, k)
            send_second(k, 1)
        for k in range(CHUNKS):
            await_odd(k)
            send_odd(0, k)

    @pl.when(col == 4)
    def _():
        for k in range(CHUNKS):
            if k == W_AT:
                pl.when(z == 0)(w_onward)
            await_odd(k)
            send_odd(4, k)
            send_second(k, 1)
        for k in range(CHUNKS):
            await_even(k)
            send_even(4, k)

    for column in (2, 6):
        @pl.when(col == column)
        def _(column=column):
            for k in range(CHUNKS):
                if k == W_AT:
                    pl.when(z == 0)(w_onward)
                await_even(k)
                send_even(column, k)
                await_odd(k)
                send_odd(column, k)
                send_second(k, 1)

    @pl.when(core == 1)
    def _():
        pl.when(z == 0)(w_onward)
        send_slab(0)
        for k in range(CHUNKS):
            await_even(k)
            await_odd(k)

    pl.when(z > 0)(w_onward)

    @pl.when(row > 0)
    def _():
        for n in range(1, 4):
            pltpu.make_async_copy(w.at[0], w.at[0], s_wy.at[n - 1]).wait()

    def multiply(k, carry):
        def product(ref):
            whole = ref[:, :, k].reshape(MEMBERS * rows, PANEL)
            return dot(whole, w[...].reshape(PANEL, PANEL)).reshape(4, 2, rows, PANEL)

        @pl.when(col == 0)
        def _():
            result[:, :, k] = product(mixed)

        @pl.when(col > 0)
        def _():
            result[:, :, k] = product(panel)

        return carry

    lax.fori_loop(0, CHUNKS, multiply, 0)

    def finish(k, carry):
        @pl.when(col > 0)
        def _():
            pltpu.make_async_copy(mixed.at[:, :, k], mixed.at[:, :, k], s_rx2.at[k]).wait()
            result[:, :, k] = mixed[:, :, k] - result[:, :, k]

        @pl.when(on_top & (k < TOP_CHUNKS))
        def _():
            result[0, 0, k] = top_out[pl.ds(pl.multiple_of(k * rows, rows), rows)]

        pltpu.make_async_copy(result.at[:, :, k], out.at[:, :, k], s_out.at[k]).start()
        return carry

    lax.fori_loop(0, CHUNKS, finish, 0)

    for column in (0, 2, 4, 6):
        @pl.when(col == column)
        def _(column=column):
            for k in range(CHUNKS):
                for copy in panel_even(column, k) + panel_odd(column, k):
                    copy.wait_send()

    seven = pl.ds(0, 7)

    def drain(k, carry):
        pltpu.make_async_copy(rx.at[k, seven], rx.at[k, seven], s_tx1.at[k]).wait()
        @pl.when(col != 4)
        def _():
            pltpu.make_async_copy(tx.at[k, seven], tx.at[k, seven], s_tx2.at[k]).wait()

        @pl.when(col == 4)
        def _():
            pltpu.make_async_copy(tx.at[k, pl.ds(0, 6)], tx.at[k, pl.ds(0, 6)], s_tx2.at[k]).wait()

        pltpu.make_async_copy(result.at[:, :, k], out.at[:, :, k], s_out.at[k]).wait()
        return carry

    lax.fori_loop(0, CHUNKS, drain, 0)
    pltpu.make_async_copy(d_recv.at[seven], d_recv.at[seven], s_d.at[1]).wait()

    @pl.when(on_top & (col < 4))
    def _():
        remote(tx.at[half, 1], top, s_aux.at[4], s_top.at[0], (row, col + 4)).wait_send()

    @pl.when(on_top)
    def _():
        spread_a00(tx.at[half, 0], wait_send)

    w_scatter(wait_send)
    w_along_z(wait_send)
    w_along_y(wait_send)


def local(window, outer_diag, inner_diag, column_diag):
    local_rows, local_cols = window.shape
    rows = local_rows // (MEMBERS * CHUNKS)
    pieces = (4, 2, CHUNKS, rows, local_cols)
    f32 = jnp.float32
    dma = pltpu.SemaphoreType.DMA
    square = pltpu.VMEM((PANEL, PANEL), f32)
    quarters = pltpu.VMEM((4, PANEL // 4, PANEL), f32)
    anywhere = pl.BlockSpec(memory_space=pl.ANY)
    factored = pl.pallas_call(
        kernel,
        out_shape=jax.ShapeDtypeStruct(pieces, f32),
        in_specs=[anywhere] * 4,
        out_specs=anywhere,
        scratch_shapes=[
            pltpu.VMEM((local_rows // LANES, LANES), f32),
            pltpu.VMEM((local_rows // LANES, LANES), f32),
            pltpu.VMEM((local_cols // LANES, LANES), f32),
            pltpu.VMEM((MEMBERS, 16, LANES), f32),
            pltpu.VMEM((MEMBERS, 16, LANES), f32),
            pltpu.VMEM((8, local_rows // MEMBERS, LANES), f32),
            pltpu.VMEM((CHUNKS, MEMBERS, rows, local_cols), f32),
            pltpu.VMEM((CHUNKS, MEMBERS, rows, local_cols), f32),
            pltpu.VMEM(pieces, f32),
            pltpu.VMEM(pieces, f32),
            pltpu.VMEM(pieces, f32),
            quarters,
            quarters,
            square,
            square,
            square,
            square,
            square,
            quarters,
            dma((2,)),
            dma((CHUNKS,)),
            dma((CHUNKS,)),
            dma((CHUNKS,)),
            dma((CHUNKS,)),
            dma((CHUNKS,)),
            dma((CHUNKS,)),
            dma((CHUNKS, 8)),
            dma((2,)),
            dma((5,)),
            dma,
            dma((3,)),
            dma((13,)),
            dma((CHUNKS,)),
            dma((3,)),
        ],
        compiler_params=pltpu.CompilerParams(
            collective_id=0, has_side_effects=True, vmem_limit_bytes=48 * 2**20
        ),
        name="butterfly_lu",
    )(
        window.reshape(pieces),
        outer_diag.reshape(local_rows // LANES, LANES),
        inner_diag.reshape(local_rows // LANES, LANES),
        column_diag.reshape(local_cols // LANES, LANES),
    )
    return factored.reshape(local_rows, local_cols)


def solution(mesh):
    in_specs = (P("row", "col"), P("row"), P("row"), P("col"))
    return jax.shard_map(
        local, mesh=mesh, in_specs=in_specs, out_specs=P("row", "col"), check_vma=False
    )
```

```python
import jax
import jax.numpy as jnp
from jax import lax
from jax.experimental import pallas as pl
from jax.experimental.pallas import tpu as pltpu
from jax.sharding import PartitionSpec as P

MESH = pl.DeviceIdType.MESH
ROOT_HALF = 0.7071067811865476
PANEL = 256
LANES = 128
MEMBERS = 8
CHUNKS = 8
W_AT = 7
TOP_CHUNKS = CHUNKS // 2
HIGHEST = lax.Precision.HIGHEST


def dot(a, b):
    return jnp.dot(a, b, precision=HIGHEST, preferred_element_type=jnp.float32)


def iota(shape, dim):
    return lax.broadcasted_iota(jnp.int32, shape, dim)


def lu_steps(lu, first, count):
    left = 0 if first < LANES else LANES
    rows, width = PANEL - first, PANEL - left
    lane = iota((1, width), 1) + left
    half_lane = iota((1, LANES), 1) + left
    row_id = iota((rows, 1), 0) + first

    def step(i, carry):
        k = first + i
        pivot_row = lu[pl.ds(k, 1)][:, left:]
        pivot = jnp.sum(jnp.where(half_lane == k, pivot_row[:, :LANES], 0.0), axis=1, keepdims=True)
        column = jnp.sum(
            jnp.where(half_lane == k, lu[first:, left : left + LANES], 0.0), axis=1, keepdims=True
        )
        factor = jnp.where(row_id > k, column / pivot, 0.0)
        lu[first:, left:] = lu[first:, left:] - factor * jnp.where(lane > k, pivot_row, 0.0)
        return carry

    lax.fori_loop(0, count, step, 0)


def invert(lu, unit_upper, low_inv, up_inv):
    i, j = iota((PANEL, PANEL), 0), iota((PANEL, PANEL), 1)
    raw = lu[...]
    diag = jnp.where(i == j, raw, 0.0)
    diag_row = jnp.sum(diag, axis=0, keepdims=True)
    diag_col = jnp.sum(diag, axis=1, keepdims=True)
    lu[...] = jnp.where(i > j, raw / diag_row, raw)
    unit_upper[...] = raw / diag_col
    eye = jnp.where(i == j, 1.0, 0.0)
    low_inv[...] = eye - jnp.where((i == j + 1) & (i % 2 == 1), lu[...], 0.0)
    up_inv[...] = eye - jnp.where((j == i + 1) & (j % 2 == 1), unit_upper[...], 0.0)

    def level(n, carry):
        bi, bj = lax.shift_right_logical(i, n), lax.shift_right_logical(j, n)
        low = jnp.where((bi == bj + 1) & (bi % 2 == 1), lu[...], 0.0)
        up = jnp.where((bj == bi + 1) & (bj % 2 == 1), unit_upper[...], 0.0)
        low_inv[...] -= dot(low_inv[...], dot(low, low_inv[...]))
        up_inv[...] -= dot(up_inv[...], dot(up, up_inv[...]))
        return carry

    lax.fori_loop(1, 8, level, 0)
    up_inv[...] = up_inv[...] / diag_row


def kernel(
    window, outer_hbm, inner_hbm, cdiag_hbm, out,
    outer, inner, cdiag, d_send, d_recv, d_wide, rx, tx, mixed, panel, result,
    top, a00, lu, unit_upper, low_inv, up_inv, top_out, w,
    s_d, s_rx1, s_tx1, s_rx2, s_tx2, s_pa, s_pb, s_ptx, s_top, s_aux, s_w, s_wy, s_wtx, s_out, s_in,
):
    row, col = lax.axis_index("row"), lax.axis_index("col")
    z, y = row // 4, row % 4
    core = col % 2
    q, xh = row // 8, col // 4
    me = q * 2 + xh
    rows = rx.shape[2]

    def member(mq, mx):
        return (row % 8 + 8 * mq, col % 4 + 4 * mx)

    def remote(src, dst, send, recv, where):
        return pltpu.make_async_remote_copy(src, dst, send, recv, device_id=where, device_id_type=MESH)

    others = [(dq, dx) for dq in range(4) for dx in range(2) if dq or dx]

    def turned_q(dq):
        return (q, q + 1 - 2 * (q % 2), (q + 2) % 4, 3 - q)[dq]

    def peer(dq, dx):
        return turned_q(dq), (xh + dx) % 2

    loads = [
        pltpu.make_async_copy(src, dst, s_in.at[n])
        for n, (src, dst) in enumerate(((outer_hbm, outer), (inner_hbm, inner), (cdiag_hbm, cdiag)))
    ]
    for load in loads:
        load.start()

    barrier = pltpu.get_barrier_semaphore()
    partners = [member(*peer(dq, dx)) for dq, dx in others]
    partners += [(row, col // 4 * 4 + (col + n) % 4) for n in range(1, 4)]
    partners += [(row, (col // 4 * 4 + 4) % 8 + (col + n) % 4) for n in range(1, 4)]
    partners += [((z + n) % 8 * 4 + y, col) for n in (1, 3, 5, 7)]
    partners += [(z * 4 + (y + n) % 4, col) for n in range(1, 4)]
    for where in partners:
        pl.semaphore_signal(barrier, inc=1, device_id=where, device_id_type=MESH)
    for load in loads:
        load.wait()
    for p in range(MEMBERS):
        d_send[p, 0:4] = outer[4 * p : 4 * p + 4] * ROOT_HALF
        d_send[p, 4:8] = inner[4 * p : 4 * p + 4] * ROOT_HALF
        d_send[p, 8:10] = cdiag[...] * ROOT_HALF
        d_send[p, 10:16] = jnp.zeros((6, LANES), jnp.float32)
    pl.semaphore_wait(barrier, len(partners))

    pltpu.make_async_copy(d_send.at[me], d_recv.at[me], s_d.at[0]).start()
    for dq, dx in others:
        mq, mx = peer(dq, dx)
        remote(d_send.at[mq * 2 + mx], d_recv.at[me], s_d.at[1], s_d.at[0], member(mq, mx)).start()

    def send_first(k):
        pltpu.make_async_copy(window.at[q, xh, k], rx.at[k, me], s_rx1.at[k]).start()
        for dq, dx in others:
            mq, mx = peer(dq, dx)
            remote(window.at[mq, mx, k], rx.at[k, me], s_tx1.at[k], s_rx1.at[k], member(mq, mx)).start()

    for k in range(CHUNKS):
        send_first(k)

    pltpu.make_async_copy(d_recv, d_recv, s_d.at[0]).wait()
    for n in range(4):
        turned = jnp.transpose(d_recv[2 * n, 0:8])
        for part in range(2):
            for b in range(4):
                lane = 4 * part + b
                d_wide[part * 4 + n, 128 * b : 128 * b + 128] = jnp.broadcast_to(
                    turned[:, lane : lane + 1], (LANES, LANES)
                )

    def mix(k):
        def tile(t, carry):
            r0 = pl.multiple_of(t * 8, 8)
            for h in range(2):
                lanes = slice(h * LANES, h * LANES + LANES)
                od = [d_wide[n, pl.ds(k * rows + r0, 8)] for n in range(4)]
                idg = [d_wide[4 + n, pl.ds(k * rows + r0, 8)] for n in range(4)]
                sides = []
                for side in range(2):
                    x = [rx[k, 2 * n + side, pl.ds(r0, 8), lanes] * od[n] for n in range(4)]
                    a = [x[0] + x[2], x[1] + x[3], x[0] - x[2], x[1] - x[3]]
                    a = [a[n] * idg[n] for n in range(4)]
                    b = [a[0] + a[1], a[0] - a[1], a[2] + a[3], a[2] - a[3]]
                    cd = d_recv[side, 8 + h : 9 + h]
                    sides.append([v * cd for v in b])
                for n in range(4):
                    tx[k, 2 * n, pl.ds(r0, 8), lanes] = sides[0][n] + sides[1][n]
                    tx[k, 2 * n + 1, pl.ds(r0, 8), lanes] = sides[0][n] - sides[1][n]
            return carry

        lax.fori_loop(0, rows // 8, tile, 0)

    panel_group = col % 4 == 0

    def send_second(k, mx):
        here = panel_group & (xh == 1) & (mx == 0)
        for dq in range(4):
            mq = turned_q(dq)
            src = tx.at[k, mq * 2 + mx]

            def far(src=src, mq=mq):
                remote(src, mixed.at[q, xh, k], s_tx2.at[k], s_rx2.at[k], member(mq, mx)).start()

            def near(src=src, mq=mq):
                remote(src, panel.at[q, xh, k], s_tx2.at[k], s_pb.at[k], member(mq, 1)).start()

            if dq:
                pl.when(here)(near)
                pl.when(jnp.logical_not(here))(far)
            else:
                pl.when((mx != xh) & jnp.logical_not(here))(far)

                @pl.when(here)
                def _(src=src):
                    pltpu.make_async_copy(src, panel.at[q, xh, k], s_pb.at[k]).start()

                @pl.when(mx == xh)
                def _(src=src):
                    pltpu.make_async_copy(src, mixed.at[q, xh, k], s_rx2.at[k]).start()

    half = pl.ds(0, TOP_CHUNKS)

    def spread_a00(src0, act):
        for column, kids in ((0, (4, 2, 6, 1)), (2, (3,)), (4, (5,)), (6, (7,))):
            @pl.when(col == column)
            def _(column=column, kids=kids):
                for n, kid in enumerate(kids):
                    act(remote(src0 if column == 0 else a00, a00, s_aux.at[n], s_top.at[1], (row, kid)))

    def start(copy):
        copy.start()

    def wait_send(copy):
        copy.wait_send()

    on_top = row == 0

    def take_a00():
        pltpu.make_async_copy(a00, a00, s_top.at[1]).wait()

        @pl.when(col > 0)
        def _():
            spread_a00(a00, start)

        lu[...] = a00[...].reshape(PANEL, PANEL)

    def solve_top():
        pltpu.make_async_copy(top, top, s_top.at[0]).wait()

        @pl.when(col == 0)
        def _():
            top_out[...] = lu[...]
            w[...] = up_inv[...].reshape(w.shape)

        @pl.when(col > 0)
        def _():
            top_out[...] = dot(low_inv[...], top[...].reshape(PANEL, PANEL))
            w[...] = dot(up_inv[...], top_out[...]).reshape(w.shape)

    def w_scatter(act):
        @pl.when(on_top)
        def _():
            for n in range(1, 4):
                act(remote(w.at[n], w.at[n], s_wtx.at[n - 1], s_w, (n, col)))

    def w_along_z(act):
        @pl.when(z == 0)
        def _():
            for n in range(1, 8):
                act(remote(w.at[y], w.at[y], s_wtx.at[2 + n], s_w, (n * 4 + y, col)))

    def w_along_y(act):
        for n in range(1, 4):
            @pl.when((z > 0) | (y != 4 - n))
            def _(n=n):
                act(remote(w.at[y], w.at[y], s_wtx.at[9 + n], s_wy.at[n - 1], (z * 4 + (y + n) % 4, col)))

    def top_rows():
        @pl.when(on_top & (col < 4))
        def _():
            remote(tx.at[half, 1], top, s_aux.at[4], s_top.at[0], (row, col + 4)).start()
            pltpu.make_async_copy(tx.at[half, 0], top, s_top.at[0]).start()

        @pl.when(on_top & (col == 0))
        def _():
            pltpu.make_async_copy(tx.at[half, 0], a00, s_top.at[1]).start()
            spread_a00(tx.at[half, 0], start)

    def w_from_top():
        invert(lu, unit_upper, low_inv, up_inv)
        solve_top()
        w_scatter(start)
        w_along_z(start)
        w_along_y(start)

    def w_onward():
        @pl.when(row > 0)
        def _():
            pltpu.make_async_copy(w.at[y], w.at[y], s_w).wait()
            w_along_z(start)
            w_along_y(start)

    def even_of(ref, k):
        return ref.at[:, 0, k]

    def odd_of(ref, k):
        return ref.at[:, 1, k]

    def panel_even(column, k):
        src = even_of(mixed if column == 0 else panel, k)
        kids = {0: (2, 6, 1), 2: (3, 4)[: 2 - k % 2], 4: (5,), 6: (7, 4)[: 1 + k % 2]}[column]
        return [remote(src, even_of(panel, k), s_ptx.at[k, n], s_pa.at[k], (row, kid)) for n, kid in enumerate(kids)]

    def panel_odd(column, k):
        src = odd_of(mixed if column == 0 else panel, k)
        kids = {0: (1,), 2: (3, 0)[: 2 - k % 2], 4: (2, 6, 5), 6: (7, 0)[: 1 + k % 2]}[column]
        return [
            remote(src, odd_of(mixed if kid == 0 else panel, k), s_ptx.at[k, 4 + n], s_pb.at[k], (row, kid))
            for n, kid in enumerate(kids)
        ]

    def await_even(k):
        pltpu.make_async_copy(even_of(panel, k), even_of(panel, k), s_pa.at[k]).wait()

    def await_odd(k):
        pltpu.make_async_copy(odd_of(panel, k), odd_of(panel, k), s_pb.at[k]).wait()

    def send_even(column, k):
        for copy in panel_even(column, k):
            copy.start()

    def send_odd(column, k):
        for copy in panel_odd(column, k):
            copy.start()

    def send_slab(mx):
        def body(k, carry):
            send_second(k, mx)
            return carry

        lax.fori_loop(0, CHUNKS, body, 0)

    for k in range(CHUNKS):
        pltpu.make_async_copy(rx.at[k], rx.at[k], s_rx1.at[k]).wait()
        mix(k)
        send_second(k, core)
        if k == TOP_CHUNKS - 1:
            top_rows()
        if k == TOP_CHUNKS:
            pl.when(on_top)(take_a00)
        if k >= TOP_CHUNKS:
            @pl.when(on_top)
            def _(k=k):
                lu_steps(lu, 64 * (k - TOP_CHUNKS), 64)

    pl.when(on_top)(w_from_top)
    @pl.when(col == 0)
    def _():
        for k in range(CHUNKS):
            if k == W_AT:
                pl.when(z == 0)(w_onward)
            pltpu.make_async_copy(even_of(mixed, k), even_of(mixed, k), s_rx2.at[k]).wait()
            send_even(0, k)
            send_second(k, 1)
        for k in range(CHUNKS):
            await_odd(k)
            send_odd(0, k)

    @pl.when(col == 4)
    def _():
        for k in range(CHUNKS):
            if k == W_AT:
                pl.when(z == 0)(w_onward)
            await_odd(k)
            send_odd(4, k)
            send_second(k, 1)
        for k in range(CHUNKS):
            await_even(k)
            send_even(4, k)

    for column in (2, 6):
        @pl.when(col == column)
        def _(column=column):
            for k in range(CHUNKS):
                if k == W_AT:
                    pl.when(z == 0)(w_onward)
                await_even(k)
                send_even(column, k)
                await_odd(k)
                send_odd(column, k)
                send_second(k, 1)

    @pl.when(core == 1)
    def _():
        for k in range(CHUNKS):
            if k == 6:
                pl.when(z == 0)(w_onward)
            send_second(k, 0)
        for k in range(CHUNKS):
            await_even(k)
            await_odd(k)

    pl.when(z > 0)(w_onward)

    @pl.when(row > 0)
    def _():
        for n in range(1, 4):
            pltpu.make_async_copy(w.at[0], w.at[0], s_wy.at[n - 1]).wait()

    def multiply(k, carry):
        def product(ref):
            whole = ref[:, :, k].reshape(MEMBERS * rows, PANEL)
            return dot(whole, w[...].reshape(PANEL, PANEL)).reshape(4, 2, rows, PANEL)

        @pl.when(col == 0)
        def _():
            result[:, :, k] = product(mixed)

        @pl.when(col > 0)
        def _():
            result[:, :, k] = product(panel)

        return carry

    lax.fori_loop(0, CHUNKS, multiply, 0)

    def finish(k, carry):
        @pl.when(col > 0)
        def _():
            pltpu.make_async_copy(mixed.at[:, :, k], mixed.at[:, :, k], s_rx2.at[k]).wait()
            result[:, :, k] = mixed[:, :, k] - result[:, :, k]

        @pl.when(on_top & (k < TOP_CHUNKS))
        def _():
            result[0, 0, k] = top_out[pl.ds(pl.multiple_of(k * rows, rows), rows)]

        pltpu.make_async_copy(result.at[:, :, k], out.at[:, :, k], s_out.at[k]).start()
        return carry

    lax.fori_loop(0, CHUNKS, finish, 0)

    for column in (0, 2, 4, 6):
        @pl.when(col == column)
        def _(column=column):
            for k in range(CHUNKS):
                for copy in panel_even(column, k) + panel_odd(column, k):
                    copy.wait_send()

    seven = pl.ds(0, 7)

    def drain(k, carry):
        pltpu.make_async_copy(rx.at[k, seven], rx.at[k, seven], s_tx1.at[k]).wait()
        @pl.when(col != 4)
        def _():
            pltpu.make_async_copy(tx.at[k, seven], tx.at[k, seven], s_tx2.at[k]).wait()

        @pl.when(col == 4)
        def _():
            pltpu.make_async_copy(tx.at[k, pl.ds(0, 6)], tx.at[k, pl.ds(0, 6)], s_tx2.at[k]).wait()

        pltpu.make_async_copy(result.at[:, :, k], out.at[:, :, k], s_out.at[k]).wait()
        return carry

    lax.fori_loop(0, CHUNKS, drain, 0)
    pltpu.make_async_copy(d_recv.at[seven], d_recv.at[seven], s_d.at[1]).wait()

    @pl.when(on_top & (col < 4))
    def _():
        remote(tx.at[half, 1], top, s_aux.at[4], s_top.at[0], (row, col + 4)).wait_send()

    @pl.when(on_top)
    def _():
        spread_a00(tx.at[half, 0], wait_send)

    w_scatter(wait_send)
    w_along_z(wait_send)
    w_along_y(wait_send)


def local(window, outer_diag, inner_diag, column_diag):
    local_rows, local_cols = window.shape
    rows = local_rows // (MEMBERS * CHUNKS)
    pieces = (4, 2, CHUNKS, rows, local_cols)
    f32 = jnp.float32
    dma = pltpu.SemaphoreType.DMA
    square = pltpu.VMEM((PANEL, PANEL), f32)
    quarters = pltpu.VMEM((4, PANEL // 4, PANEL), f32)
    anywhere = pl.BlockSpec(memory_space=pl.ANY)
    factored = pl.pallas_call(
        kernel,
        out_shape=jax.ShapeDtypeStruct(pieces, f32),
        in_specs=[anywhere] * 4,
        out_specs=anywhere,
        scratch_shapes=[
            pltpu.VMEM((local_rows // LANES, LANES), f32),
            pltpu.VMEM((local_rows // LANES, LANES), f32),
            pltpu.VMEM((local_cols // LANES, LANES), f32),
            pltpu.VMEM((MEMBERS, 16, LANES), f32),
            pltpu.VMEM((MEMBERS, 16, LANES), f32),
            pltpu.VMEM((8, local_rows // MEMBERS, LANES), f32),
            pltpu.VMEM((CHUNKS, MEMBERS, rows, local_cols), f32),
            pltpu.VMEM((CHUNKS, MEMBERS, rows, local_cols), f32),
            pltpu.VMEM(pieces, f32),
            pltpu.VMEM(pieces, f32),
            pltpu.VMEM(pieces, f32),
            quarters,
            quarters,
            square,
            square,
            square,
            square,
            square,
            quarters,
            dma((2,)),
            dma((CHUNKS,)),
            dma((CHUNKS,)),
            dma((CHUNKS,)),
            dma((CHUNKS,)),
            dma((CHUNKS,)),
            dma((CHUNKS,)),
            dma((CHUNKS, 8)),
            dma((2,)),
            dma((5,)),
            dma,
            dma((3,)),
            dma((13,)),
            dma((CHUNKS,)),
            dma((3,)),
        ],
        compiler_params=pltpu.CompilerParams(
            collective_id=0, has_side_effects=True, vmem_limit_bytes=48 * 2**20
        ),
        name="butterfly_lu",
    )(
        window.reshape(pieces),
        outer_diag.reshape(local_rows // LANES, LANES),
        inner_diag.reshape(local_rows // LANES, LANES),
        column_diag.reshape(local_cols // LANES, LANES),
    )
    return factored.reshape(local_rows, local_cols)


def solution(mesh):
    in_specs = (P("row", "col"), P("row"), P("row"), P("col"))
    return jax.shard_map(
        local, mesh=mesh, in_specs=in_specs, out_specs=P("row", "col"), check_vma=False
    )
```
